32 devices in a mesh: row: 4 (over x, core), col: 8 (over z, y).
Axes of the slice: x: 2, y: 2, z: 4, core: 2. Of those that a mesh axis runs over, the one named last changes fastest.
Arguments:
- features: bfloat16 [4096, 768], P(('row', 'col')), may hold values from -6 to 6
- self_weight: bfloat16 [768, 768], replicated, may hold values from -0.21875 to 0.21875
- rel_weight: bfloat16 [768, 5, 768], replicated, may hold values from -0.21875 to 0.21875
- bias: float32 [768], replicated, may hold values from -3 to 3
- blocks: bfloat16 [4, 8, 5, 8, 128, 128], P('row', 'col'), may hold values from -0.083496094 to 0.083496094
- block_rows: int32 [4, 8, 5, 8], P('row', 'col'), may hold values from 0 to 7
- block_cols: int32 [4, 8, 5, 8], P('row', 'col'), may hold values from 0 to 3
- block_counts: int32 [4, 8, 5], P('row', 'col'), may hold values from 1 to 8, as said below
Outputs:
- layer_out: bfloat16 [4096, 768], P(('row', 'col'))
The draws below stay inside these ranges and needn't reach their ends.
Inputs may be any that keep to these rules, and one draw needn't show every extreme that they name: The live slots of a tile and relation are its first block_counts slots; the others are ignored. `block_rows`: pairs of destination and source blocks may repeat within a tile.
All inputs are finite; a program needn't handle non-finite values.
Results may differ from the reference program's by a relative error of at most 0.014.
Values may be sent and summed in bfloat16 or wider, within the bound.
A program may use at most 128 MiB of HBM per device.

```python
import jax
import jax.numpy as jnp
from jax import lax

D = 768
REL = 5
BLOCK = 128
ROWS_DEV = 128
SLOTS = 8
NODES = 4096
BROWS = 8
BCOLS = 4
N_ROW = 4
N_COL = 8


def draw_block_counts(key, part):
    first_key, second_key = jax.random.split(jax.random.fold_in(key, 17))
    total = N_ROW * N_COL * REL
    spread = jax.random.randint(first_key, (total,), 0, SLOTS)
    counts = 1 + spread * spread // SLOTS
    chosen = jax.random.randint(second_key, (), 0, total)
    counts = jnp.where(jnp.arange(total) == chosen, SLOTS, counts)
    return counts.reshape(N_ROW, N_COL, REL).astype(jnp.int32)


def plant(drawn, rng, smallest, largest):
    index_at = [jax.random.randint(jax.random.fold_in(rng, axis), (), 0, length) for axis, length in enumerate(drawn.shape)]
    main_axis = drawn.shape.index(max(drawn.shape))
    neighbour = index_at[:main_axis] + [(index_at[main_axis] + 1) % drawn.shape[main_axis]] + index_at[main_axis + 1:]
    return drawn.at[tuple(index_at)].set(smallest).at[tuple(neighbour)].set(largest)


def level_of(rng, extent, cuts, least, high):
    loudness = 1.0
    for dim, blocks in cuts:
        heights = jax.random.uniform(jax.random.fold_in(jax.random.fold_in(rng, 6), dim), (blocks,), jnp.float32, least / len(cuts), high / len(cuts))
        loudness = loudness * jnp.repeat(jnp.exp(heights), extent[dim] // blocks).reshape((-1,) + (1,) * (len(extent) - 1 - dim))
    return loudness


def bell_draw(stream_key, dims, deviation, most, cuts=(), kind=jnp.bfloat16):
    result = jax.random.normal(stream_key, dims, jnp.float32) * deviation
    if len(cuts) > 0:
        result = level_of(stream_key, dims, cuts, -0.22, 0.18) * result
    return jnp.clip(result, min=-most, max=most).astype(kind)


def setup_inputs(seed: int = 0) -> dict:
    arg_keys = jax.random.split(jax.random.key(seed), 9)
    features = bell_draw(arg_keys[0], (NODES, D), 1.0, 6.0, ((0, 32),))
    self_weight = bell_draw(arg_keys[1], (D, D), D ** -0.5, 0.21875)
    rel_weight = bell_draw(arg_keys[2], (D, REL, D), D ** -0.5, 0.21875)
    bias = bell_draw(arg_keys[3], (D,), 0.5, 3.0, (), jnp.float32)
    blocks = bell_draw(arg_keys[4], (N_ROW, N_COL, REL, SLOTS, BLOCK, BLOCK), ((ROWS_DEV / (SLOTS * REL)) ** 0.5 / BLOCK), 0.083496094, ((0, 4), (1, 8)))
    block_rows = plant(jax.random.randint(arg_keys[5], (N_ROW, N_COL, REL, SLOTS), 0, BROWS), jax.random.fold_in(arg_keys[5], 1), 0, BROWS - 1).astype(jnp.int32)
    block_cols = plant(jax.random.randint(arg_keys[6], (N_ROW, N_COL, REL, SLOTS), 0, BCOLS), jax.random.fold_in(arg_keys[6], 1), 0, BCOLS - 1).astype(jnp.int32)
    block_counts = draw_block_counts(jax.random.fold_in(arg_keys[8], 71), 0)
    return {"features": features, "self_weight": self_weight, "rel_weight": rel_weight, "bias": bias, "blocks": blocks, "block_rows": block_rows, "block_cols": block_cols, "block_counts": block_counts}


def tile_sum(tile_blocks, tile_rows, tile_cols, tile_counts, panel):
    slots = tile_blocks.shape[1]
    width = panel.shape[-1]
    total = jnp.zeros((BROWS, BLOCK, width), jnp.float32)
    for relation in range(REL):
        source = panel[:, :, relation, :]
        chosen = source[tile_cols[relation]]
        live = (jnp.arange(slots, dtype=jnp.int32) < tile_counts[relation]).astype(jnp.float32)
        owners = (tile_rows[relation][None, :] == jnp.arange(BROWS, dtype=jnp.int32)[:, None]).astype(jnp.float32) * live[None, :]
        products = jnp.einsum("sik,skd->sid", tile_blocks[relation].astype(jnp.float32), chosen.astype(jnp.float32))
        total = total + jnp.einsum("ns,sid->nid", owners, products, precision=lax.Precision.HIGHEST)
    rounded = lax.optimization_barrier(total.astype(jnp.bfloat16))
    return rounded.astype(jnp.float32).reshape(BROWS * BLOCK, width)


def reference(features, self_weight, rel_weight, bias, blocks, block_rows, block_cols, block_counts):
    nodes, width = features.shape
    stacked = rel_weight.reshape(width, REL * width)
    transformed = jnp.dot(features, stacked, preferred_element_type=jnp.float32).astype(jnp.bfloat16)
    grouped = transformed.reshape(N_ROW, N_COL, ROWS_DEV, REL, width)

    def row_group(inputs):
        group_blocks, group_rows, group_cols, group_counts = inputs

        def step(total, item):
            column, one_blocks, one_rows, one_cols, one_counts = item
            panel = lax.dynamic_index_in_dim(grouped, column, axis=1, keepdims=False)
            panel = panel.reshape(BCOLS, BLOCK, REL, width)
            return total + tile_sum(one_blocks, one_rows, one_cols, one_counts, panel), None

        init = jnp.zeros((BROWS * BLOCK, width), jnp.float32)
        columns = jnp.arange(N_COL, dtype=jnp.int32)
        total, _ = lax.scan(step, init, (columns, group_blocks, group_rows, group_cols, group_counts))
        return total

    aggregate = lax.map(row_group, (blocks, block_rows, block_cols, block_counts))
    aggregate = aggregate.reshape(nodes, width)
    self_term = jnp.dot(features, self_weight, preferred_element_type=jnp.float32)
    return jnp.maximum(self_term + aggregate + bias, 0.0).astype(jnp.bfloat16)
```

```python
import functools

import jax
import jax.numpy as jnp
from jax import lax
from jax.experimental import pallas as pl
from jax.experimental.pallas import tpu as pltpu
from jax.sharding import PartitionSpec as P

MESH = pl.DeviceIdType.MESH


def flip(index, mask):
    out = index
    bit = 1
    while bit <= mask:
        if mask & bit:
            out = out + bit - 2 * bit * lax.rem(lax.div(index, bit), 2)
        bit *= 2
    return out


def xor(left, right, size):
    out = 0
    bit = 1
    while bit < size:
        out = out + bit * lax.rem(lax.div(left, bit) + lax.div(right, bit), 2)
        bit *= 2
    return out


def layer_kernel(
    n_row, n_col,
    feat, rows, cols, counts, bias, rel_hbm, self_hbm, blocks_hbm,
    out,
    xbuf, wbuf, swbuf, bbuf, merged, panel, lhs, idx, pairs, own, self_sum, sends, recvs,
    w_sem, sw_sem, b_sem, ag_send, ag_recv, fw_send, fw_recv, rs_send, rs_recv,
):
    block, width = feat.shape
    relations = rel_hbm.shape[0]
    slots = blocks_hbm.shape[0] // relations
    n_pair = n_row // 2
    half = n_col // 2
    n_src = n_row * block
    me_row = lax.axis_index("row")
    me_col = lax.axis_index("col")
    sibling = flip(me_row, 1)
    me_pair = lax.div(me_row, 2)

    b_copy = pltpu.make_async_copy(blocks_hbm, bbuf, b_sem)
    b_copy.start()
    w_copies = []
    for r in range(relations):
        copy = pltpu.make_async_copy(rel_hbm.at[r], wbuf.at[r], w_sem.at[r])
        copy.start()
        w_copies.append(copy)
    sw_copy = pltpu.make_async_copy(self_hbm, swbuf, sw_sem)
    sw_copy.start()

    barrier = pltpu.get_barrier_semaphore()
    row_peers = [sibling] + [flip(me_row, 2 * j) for j in range(1, n_pair)]
    masks = []
    while 2 ** len(masks) < n_col:
        masks.append(2 ** len(masks))
    for peer in row_peers:
        pl.semaphore_signal(barrier, inc=1, device_id={"row": peer}, device_id_type=MESH)
    for mask in masks:
        pl.semaphore_signal(
            barrier, inc=1, device_id={"col": flip(me_col, mask)}, device_id_type=MESH
        )
    pl.semaphore_wait(barrier, len(row_peers) + len(masks))

    def span(row):
        return xbuf.at[pl.ds(pl.multiple_of(row * block, block), block)]

    ag = []
    for j in list(range(1, n_pair)) + [0]:
        copy = pltpu.make_async_remote_copy(
            src_ref=feat, dst_ref=span(me_row), send_sem=ag_send.at[j], recv_sem=ag_recv.at[j],
            device_id={"row": row_peers[j]}, device_id_type=MESH,
        )
        copy.start()
        ag.append(copy)
    ag = [ag[-1]] + ag[:-1]
    xbuf[pl.ds(pl.multiple_of(me_row * block, block), block), :] = feat[...]

    def index_relation(r, carry):
        found = []
        for s in range(slots):
            pair = jnp.where(s < counts[r], rows[r, s] * n_row + cols[r, s], -1)
            found.append(pair)
            pairs[r, s] = pair

        def index_dest(d, inner):
            for k in range(n_row):
                chosen = relations * slots
                for s in range(slots):
                    chosen = jnp.where(found[s] == d * n_row + k, r * slots + s, chosen)
                idx[d, r * n_row + k] = chosen
            return inner

        return lax.fori_loop(0, n_col, index_dest, carry)

    lax.fori_loop(0, relations, index_relation, 0)
    b_copy.wait()
    merged[relations * slots] = jnp.zeros((block, block), merged.dtype)

    def merge_relation(r, carry):
        for s in range(slots):
            total = bbuf[r * slots + s].astype(jnp.float32)
            for t in range(s):
                same = jnp.where(pairs[r, s] == pairs[r, t], 1.0, 0.0).astype(jnp.float32)
                total = total + same * bbuf[r * slots + t].astype(jnp.float32)
            merged[r * slots + s] = total.astype(merged.dtype)
        return carry

    lax.fori_loop(0, relations, merge_relation, 0)

    def transform(pair):
        at = pl.multiple_of(pair * 2 * block, 2 * block)

        def one(r, carry):
            product = jnp.dot(
                xbuf[pl.ds(at, 2 * block), :], wbuf[r], preferred_element_type=jnp.float32
            )
            to = pl.multiple_of(r * n_src + at, 2 * block)
            panel[pl.ds(to, 2 * block), :] = product.astype(panel.dtype)
            return carry

        lax.fori_loop(0, relations, one, 0)

    for copy in w_copies:
        copy.wait()
    ag[0].wait_recv()
    transform(me_pair)
    sw_copy.wait()
    self_sum[...] = (
        jnp.dot(feat[...], swbuf[...], preferred_element_type=jnp.float32) + bias[...]
    )
    forwards = []
    for j in range(1, n_pair):
        ag[j].wait_recv()
        peer = row_peers[j]
        copy = pltpu.make_async_remote_copy(
            src_ref=span(peer), dst_ref=span(peer), send_sem=fw_send.at[j], recv_sem=fw_recv.at[j],
            device_id={"row": sibling}, device_id_type=MESH,
        )
        copy.start()
        forwards.append(copy)
    for j in range(1, n_pair):
        forwards[j - 1].wait_recv()
        transform(lax.div(row_peers[j], 2))

    def partial_sum(e):
        dest = xor(e, me_col, n_col)
        for k in range(relations * n_row):
            lhs[:, k * block:(k + 1) * block] = merged[idx[dest, k]]
        return jnp.dot(lhs[...], panel[...], preferred_element_type=jnp.float32)

    base = [0]
    for _ in masks:
        base.append(base[-1] + (half >> (len(base) - 1)))

    def exchange(stage, slot):
        at = base[stage] + slot
        return pltpu.make_async_remote_copy(
            src_ref=sends.at[at], dst_ref=recvs.at[at],
            send_sem=rs_send.at[at], recv_sem=rs_recv.at[at],
            device_id={"col": flip(me_col, masks[stage])}, device_id_type=MESH,
        )

    def far(t, carry):
        sends[t] = partial_sum(n_col - 1 - 2 * t).astype(sends.dtype)
        exchange(0, t).start()
        return carry

    def near(t, carry):
        own[t] = partial_sum(n_col - 2 - 2 * t)
        return carry

    lax.fori_loop(0, half, far, 0)
    lax.fori_loop(0, half, near, 0)

    for t in range(half):
        exchange(0, t).wait_recv()
        total = own[t] + recvs[t].astype(jnp.float32)
        stage, slot = 1, t
        while stage < len(masks) and slot % 2 == 1:
            slot = slot // 2
            exchange(stage, slot).wait_recv()
            total = total + recvs[base[stage] + slot].astype(jnp.float32)
            stage += 1
        if stage < len(masks):
            sends[base[stage] + slot // 2] = total.astype(sends.dtype)
            exchange(stage, slot // 2).start()
        else:
            out[...] = jnp.maximum(self_sum[...] + total, 0.0).astype(out.dtype)

    for copy in ag + forwards:
        copy.wait_send()
    for stage in range(len(masks)):
        for slot in range(half >> stage):
            exchange(stage, slot).wait_send()


def per_device(
    n_row, n_col,
    features, self_weight, rel_weight, bias, blocks, block_rows, block_cols, block_counts,
):
    block, width = features.shape
    relations = rel_weight.shape[1]
    slots = blocks.shape[3]
    size = blocks.shape[-1]
    bf16, f32, i32 = jnp.bfloat16, jnp.float32, jnp.int32
    vmem = pl.BlockSpec(memory_space=pltpu.VMEM)
    smem = pl.BlockSpec(memory_space=pltpu.SMEM)
    hbm = pl.BlockSpec(memory_space=pl.ANY)
    dma = pltpu.SemaphoreType.DMA
    n_src = n_row * block
    n_pair = n_row // 2
    flops = 2 * width * (n_src * relations * width + block * width)
    flops += 2 * n_col * block * relations * n_src * width
    return pl.pallas_call(
        functools.partial(layer_kernel, n_row, n_col),
        out_shape=jax.ShapeDtypeStruct((block, width), bf16),
        in_specs=[vmem, smem, smem, smem, vmem, hbm, hbm, hbm],
        out_specs=vmem,
        scratch_shapes=[
            pltpu.VMEM((n_src, width), bf16),
            pltpu.VMEM((relations, width, width), bf16),
            pltpu.VMEM((width, width), bf16),
            pltpu.VMEM((relations * slots, size, size), bf16),
            pltpu.VMEM((relations * slots + 1, size, size), bf16),
            pltpu.VMEM((relations * n_src, width), bf16),
            pltpu.VMEM((block, relations * n_src), bf16),
            pltpu.SMEM((n_col, relations * n_row), i32),
            pltpu.SMEM((relations, slots), i32),
            pltpu.VMEM((n_col // 2, block, width), f32),
            pltpu.VMEM((block, width), f32),
            pltpu.VMEM((n_col - 1, block, width), bf16),
            pltpu.VMEM((n_col - 1, block, width), bf16),
            dma((relations,)), dma, dma,
            dma((n_pair,)), dma((n_pair,)), dma((n_pair,)), dma((n_pair,)),
            dma((n_col - 1,)), dma((n_col - 1,)),
        ],
        compiler_params=pltpu.CompilerParams(
            collective_id=0, has_side_effects=True, vmem_limit_bytes=56 * 2 ** 20
        ),
        cost_estimate=pl.CostEstimate(flops=flops, bytes_accessed=9 * 2 ** 20, transcendentals=0),
        name="relational_layer",
    )(
        features, block_rows[0, 0], block_cols[0, 0], block_counts[0, 0], bias.reshape(1, width),
        jnp.transpose(rel_weight, (1, 0, 2)), self_weight,
        blocks.reshape(relations * slots, size, size),
    )


def solution(mesh):
    return jax.shard_map(
        functools.partial(per_device, mesh.shape["row"], mesh.shape["col"]),
        mesh=mesh,
        in_specs=(
            P(("row", "col"), None),
            P(),
            P(),
            P(),
            P("row", "col", None, None, None, None),
            P("row", "col", None, None),
            P("row", "col", None, None),
            P("row", "col", None),
        ),
        out_specs=P(("row", "col"), None),
        check_vma=False,
    )
```

```python
import functools

import jax
import jax.numpy as jnp
from jax import lax
from jax.experimental import pallas as pl
from jax.experimental.pallas import tpu as pltpu
from jax.sharding import PartitionSpec as P

MESH = pl.DeviceIdType.MESH


def flip(index, mask):
    out = index
    bit = 1
    while bit <= mask:
        if mask & bit:
            out = out + bit - 2 * bit * lax.rem(lax.div(index, bit), 2)
        bit *= 2
    return out


def xor(left, right, size):
    out = 0
    bit = 1
    while bit < size:
        out = out + bit * lax.rem(lax.div(left, bit) + lax.div(right, bit), 2)
        bit *= 2
    return out


def layer_kernel(
    n_row, n_col,
    feat, rows, cols, counts, bias, rel_hbm, self_hbm, blocks_hbm,
    out,
    xbuf, wbuf, swbuf, bbuf, merged, panel, lhs, idx, pairs, own, self_sum, sends, recvs,
    w_sem, sw_sem, b_sem, ag_send, ag_recv, fw_send, fw_recv, rs_send, rs_recv,
):
    block, width = feat.shape
    relations = rel_hbm.shape[0]
    slots = blocks_hbm.shape[0] // relations
    n_pair = n_row // 2
    half = n_col // 2
    n_src = n_row * block
    parts, _, part = panel.shape
    me_row = lax.axis_index("row")
    me_col = lax.axis_index("col")
    sibling = flip(me_row, 1)
    me_pair = lax.div(me_row, 2)

    b_copy = pltpu.make_async_copy(blocks_hbm, bbuf, b_sem)
    b_copy.start()
    w_copies = []
    for r in range(relations):
        copy = pltpu.make_async_copy(rel_hbm.at[r], wbuf.at[r], w_sem.at[r])
        copy.start()
        w_copies.append(copy)
    sw_copy = pltpu.make_async_copy(self_hbm, swbuf, sw_sem)
    sw_copy.start()

    barrier = pltpu.get_barrier_semaphore()
    row_peers = [sibling] + [flip(me_row, 2 * j) for j in range(1, n_pair)]
    masks = []
    while 2 ** len(masks) < n_col:
        masks.append(2 ** len(masks))
    for peer in row_peers:
        pl.semaphore_signal(barrier, inc=1, device_id={"row": peer}, device_id_type=MESH)
    for mask in masks:
        pl.semaphore_signal(
            barrier, inc=1, device_id={"col": flip(me_col, mask)}, device_id_type=MESH
        )
    pl.semaphore_wait(barrier, len(row_peers) + len(masks))

    def span(row):
        return xbuf.at[pl.ds(pl.multiple_of(row * block, block), block)]

    ag = []
    for j in list(range(1, n_pair)) + [0]:
        copy = pltpu.make_async_remote_copy(
            src_ref=feat, dst_ref=span(me_row), send_sem=ag_send.at[j], recv_sem=ag_recv.at[j],
            device_id={"row": row_peers[j]}, device_id_type=MESH,
        )
        copy.start()
        ag.append(copy)
    ag = [ag[-1]] + ag[:-1]
    xbuf[pl.ds(pl.multiple_of(me_row * block, block), block), :] = feat[...]

    def index_relation(r, carry):
        found = []
        for s in range(slots):
            pair = jnp.where(s < counts[0, r], rows[r, 0, s] * n_row + cols[r, 0, s], -1)
            found.append(pair)
            pairs[r, s] = pair

        def index_dest(d, inner):
            for k in range(n_row):
                chosen = relations * slots
                for s in range(slots):
                    chosen = jnp.where(found[s] == d * n_row + k, r * slots + s, chosen)
                idx[d, r * n_row + k] = chosen
            return inner

        return lax.fori_loop(0, n_col, index_dest, carry)

    lax.fori_loop(0, relations, index_relation, 0)

    def transform(pair, first, many):
        at = pl.multiple_of(pair * 2 * block, 2 * block)

        def one(r, carry):
            product = jnp.dot(
                xbuf[pl.ds(at, 2 * block), :],
                wbuf[r, :, first * part:(first + many) * part],
                preferred_element_type=jnp.float32,
            ).astype(panel.dtype)
            to = pl.multiple_of(r * n_src + at, 2 * block)
            for p in range(many):
                panel[first + p, pl.ds(to, 2 * block), :] = product[:, p * part:(p + 1) * part]
            return carry

        lax.fori_loop(0, relations, one, 0)

    for copy in w_copies:
        copy.wait()
    ag[0].wait_recv()
    transform(me_pair, 0, parts)
    forwards = []
    for j in range(1, n_pair):
        ag[j].wait_recv()
        peer = row_peers[j]
        copy = pltpu.make_async_remote_copy(
            src_ref=span(peer), dst_ref=span(peer), send_sem=fw_send.at[j], recv_sem=fw_recv.at[j],
            device_id={"row": sibling}, device_id_type=MESH,
        )
        copy.start()
        forwards.append(copy)

    sw_copy.wait()
    self_sum[...] = (
        jnp.dot(feat[...], swbuf[...], preferred_element_type=jnp.float32)
        + bias[...].reshape(1, width)
    )
    b_copy.wait()
    merged[relations * slots] = jnp.zeros((block, block), merged.dtype)

    def merge_relation(r, carry):
        for s in range(slots):
            total = bbuf[r * slots + s].astype(jnp.float32)
            for t in range(s):
                same = jnp.where(pairs[r, s] == pairs[r, t], 1.0, 0.0).astype(jnp.float32)
                total = total + same * bbuf[r * slots + t].astype(jnp.float32)
            merged[r * slots + s] = total.astype(merged.dtype)
        return carry

    lax.fori_loop(0, relations, merge_relation, 0)

    orders = [list(masks) for _ in range(parts)]
    orders[1][:2] = [masks[1], masks[0]]

    def pair_of_sums(p, v, buf):
        for h in range(2):
            e = sum(
                mask * lax.rem(lax.div(v - 2 * h, 2 ** stage), 2)
                for stage, mask in enumerate(orders[p])
            )
            dest = xor(e, me_col, n_col)
            for k in range(relations * n_row):
                lhs[buf, h * block:(h + 1) * block, k * block:(k + 1) * block] = merged[idx[dest, k]]
        return jnp.dot(lhs[buf], panel[p], preferred_element_type=jnp.float32)

    base = [0]
    for _ in masks:
        base.append(base[-1] + (half >> (len(base) - 1)))

    def exchange(p, stage, slot):
        at = base[stage] + slot
        return pltpu.make_async_remote_copy(
            src_ref=sends.at[p, at], dst_ref=recvs.at[p, at],
            send_sem=rs_send.at[p, at], recv_sem=rs_recv.at[p, at],
            device_id={"col": flip(me_col, orders[p][stage])}, device_id_type=MESH,
        )

    def receive(p, stage, slot):
        exchange(p, stage, slot).wait_recv()
        return recvs[p, base[stage] + slot].astype(jnp.float32)

    def send(p, stage, slot, total):
        sends[p, base[stage] + slot] = total.astype(sends.dtype)
        exchange(p, stage, slot).start()

    for j in range(1, n_pair):
        forwards[j - 1].wait_recv()
    for p in range(parts):
        for j in range(1, n_pair):
            transform(lax.div(row_peers[j], 2), p, 1)

        def far(i, carry):
            sums = pair_of_sums(p, n_col - 1 - 4 * i, 0)
            for h in range(2):
                send(p, 0, 2 * i + h, sums[h * block:(h + 1) * block])
            return carry

        lax.fori_loop(0, half // 2, far, 0)

    def near(p, i):
        sums = pair_of_sums(p, n_col - 2 - 4 * i, (p + i) % 2)
        send(p, 1, i, sums[:block] + receive(p, 0, 2 * i))
        own[p, i] = sums[block:] + receive(p, 0, 2 * i + 1)

    def deeper(p, i):
        total = own[p, i] + receive(p, 1, i)
        stage, slot = 2, i
        while stage < len(masks) and slot % 2 == 1:
            slot = slot // 2
            total = total + receive(p, stage, slot)
            stage += 1
        if stage < len(masks):
            send(p, stage, slot // 2, total)
        else:
            at = slice(p * part, (p + 1) * part)
            out[:, at] = jnp.maximum(self_sum[:, at] + total, 0.0).astype(out.dtype)

    last = half // 2 - 1
    for i in range(last + 1):
        near(0, i)
        near(1, i)
        if i < last:
            deeper(0, i)
            deeper(1, i)
    for p in range(2, parts):
        for i in range(last + 1):
            near(p, i)
            if p == 2 and i == 0:
                deeper(0, last)
                deeper(1, last)
            deeper(p, i)

    for copy in ag + forwards:
        copy.wait_send()
    for p in range(parts):
        for stage in range(len(masks)):
            for slot in range(half >> stage):
                exchange(p, stage, slot).wait_send()


def per_device(
    n_row, n_col,
    features, self_weight, rel_weight, bias, blocks, block_rows, block_cols, block_counts,
):
    block, width = features.shape
    relations = rel_weight.shape[1]
    slots = blocks.shape[3]
    size = blocks.shape[-1]
    bf16, f32, i32 = jnp.bfloat16, jnp.float32, jnp.int32
    vmem = pl.BlockSpec(memory_space=pltpu.VMEM)
    smem = pl.BlockSpec(memory_space=pltpu.SMEM)
    hbm = pl.BlockSpec(memory_space=pl.ANY)
    dma = pltpu.SemaphoreType.DMA
    n_src = n_row * block
    n_pair = n_row // 2
    part = 256
    parts = width // part
    flops = 2 * width * (n_src * relations * width + block * width)
    flops += 2 * n_col * block * relations * n_src * width
    return pl.pallas_call(
        functools.partial(layer_kernel, n_row, n_col),
        out_shape=jax.ShapeDtypeStruct((block, width), bf16),
        in_specs=[vmem, smem, smem, smem, vmem, hbm, hbm, hbm],
        out_specs=vmem,
        scratch_shapes=[
            pltpu.VMEM((n_src, width), bf16),
            pltpu.VMEM((relations, width, width), bf16),
            pltpu.VMEM((width, width), bf16),
            pltpu.VMEM((relations * slots, size, size), bf16),
            pltpu.VMEM((relations * slots + 1, size, size), bf16),
            pltpu.VMEM((parts, relations * n_src, part), bf16),
            pltpu.VMEM((2, 2 * block, relations * n_src), bf16),
            pltpu.SMEM((n_col, relations * n_row), i32),
            pltpu.SMEM((relations, slots), i32),
            pltpu.VMEM((parts, n_col // 4, block, part), f32),
            pltpu.VMEM((block, width), f32),
            pltpu.VMEM((parts, n_col - 1, block, part), bf16),
            pltpu.VMEM((parts, n_col - 1, block, part), bf16),
            dma((relations,)), dma, dma,
            dma((n_pair,)), dma((n_pair,)), dma((n_pair,)), dma((n_pair,)),
            dma((parts, n_col - 1)), dma((parts, n_col - 1)),
        ],
        compiler_params=pltpu.CompilerParams(
            collective_id=0, has_side_effects=True, vmem_limit_bytes=56 * 2 ** 20
        ),
        cost_estimate=pl.CostEstimate(flops=flops, bytes_accessed=9 * 2 ** 20, transcendentals=0),
        name="relational_layer",
    )(
        features, block_rows.reshape(relations, 1, slots), block_cols.reshape(relations, 1, slots),
        block_counts.reshape(1, relations), bias,
        jnp.transpose(rel_weight, (1, 0, 2)), self_weight,
        blocks.reshape(relations * slots, size, size),
    )


def solution(mesh):
    return jax.shard_map(
        functools.partial(per_device, mesh.shape["row"], mesh.shape["col"]),
        mesh=mesh,
        in_specs=(
            P(("row", "col"), None),
            P(),
            P(),
            P(),
            P("row", "col", None, None, None, None),
            P("row", "col", None, None),
            P("row", "col", None, None),
            P("row", "col", None),
        ),
        out_specs=P(("row", "col"), None),
        check_vma=False,
    )
```

```python
import functools

import jax
import jax.numpy as jnp
from jax import lax
from jax.experimental import pallas as pl
from jax.experimental.pallas import tpu as pltpu
from jax.sharding import PartitionSpec as P

MESH = pl.DeviceIdType.MESH


def flip(index, mask):
    out = index
    bit = 1
    while bit <= mask:
        if mask & bit:
            out = out + bit - 2 * bit * lax.rem(lax.div(index, bit), 2)
        bit *= 2
    return out


def xor(left, right, size):
    out = 0
    bit = 1
    while bit < size:
        out = out + bit * lax.rem(lax.div(left, bit) + lax.div(right, bit), 2)
        bit *= 2
    return out


def layer_kernel(
    n_row, n_col,
    feat, rows, cols, counts, bias, rel_hbm, self_hbm, blocks_hbm,
    out,
    xbuf, wbuf, swbuf, bbuf, merged, panel, lhs, table, idx, pairs, own, self_sum, sends, recvs,
    w_sem, sw_sem, b_sem, idx_sem, ag_send, ag_recv, fw_send, fw_recv, rs_send, rs_recv,
):
    block, width = feat.shape
    relations = rel_hbm.shape[0]
    slots = blocks_hbm.shape[0] // relations
    n_pair = n_row // 2
    half = n_col // 2
    n_src = n_row * block
    parts, _, part = panel.shape
    me_row = lax.axis_index("row")
    me_col = lax.axis_index("col")
    sibling = flip(me_row, 1)
    me_pair = lax.div(me_row, 2)

    barrier = pltpu.get_barrier_semaphore()
    row_peers = [sibling] + [flip(me_row, 2 * j) for j in range(1, n_pair)]
    masks = []
    while 2 ** len(masks) < n_col:
        masks.append(2 ** len(masks))
    for peer in row_peers:
        pl.semaphore_signal(barrier, inc=1, device_id={"row": peer}, device_id_type=MESH)
    for mask in masks:
        pl.semaphore_signal(
            barrier, inc=1, device_id={"col": flip(me_col, mask)}, device_id_type=MESH
        )
    b_copy = pltpu.make_async_copy(blocks_hbm, bbuf, b_sem)
    b_copy.start()
    w_copies = []
    for r in range(relations):
        copy = pltpu.make_async_copy(rel_hbm.at[r], wbuf.at[r], w_sem.at[r])
        copy.start()
        w_copies.append(copy)
    sw_copy = pltpu.make_async_copy(self_hbm, swbuf, sw_sem)
    sw_copy.start()

    pl.semaphore_wait(barrier, len(row_peers) + len(masks))

    def span(row):
        return xbuf.at[pl.ds(pl.multiple_of(row * block, block), block)]

    ag = []
    for j in list(range(1, n_pair)) + [0]:
        copy = pltpu.make_async_remote_copy(
            src_ref=feat, dst_ref=span(me_row), send_sem=ag_send.at[j], recv_sem=ag_recv.at[j],
            device_id={"row": row_peers[j]}, device_id_type=MESH,
        )
        copy.start()
        ag.append(copy)
    ag = [ag[-1]] + ag[:-1]
    xbuf[pl.ds(pl.multiple_of(me_row * block, block), block), :] = feat[...]

    lane = lax.broadcasted_iota(jnp.int32, table.shape, 1)
    dest_row = lax.broadcasted_iota(jnp.int32, table.shape, 0)
    lane_relation = lax.div(lane, n_row)
    wanted = (lane_relation * n_col + dest_row) * n_row + lax.rem(lane, n_row)
    chosen = jnp.full(table.shape, relations * slots, jnp.int32)
    for r in range(relations):
        for s in range(slots):
            pair = (r * n_col + rows[r, 0, s]) * n_row + cols[r, 0, s]
            pair = jnp.where(s < counts[0, r], pair, -1)
            pairs[r, s] = pair
            chosen = jnp.where(wanted == pair, r * slots + s, chosen)
    table[...] = chosen
    idx_copy = pltpu.make_async_copy(table, idx, idx_sem)
    idx_copy.start()

    def transform(pair, first, many):
        at = pl.multiple_of(pair * 2 * block, 2 * block)

        def one(r, carry):
            product = jnp.dot(
                xbuf[pl.ds(at, 2 * block), :],
                wbuf[r, :, first * part:(first + many) * part],
                preferred_element_type=jnp.float32,
            ).astype(panel.dtype)
            to = pl.multiple_of(r * n_src + at, 2 * block)
            for p in range(many):
                panel[first + p, pl.ds(to, 2 * block), :] = product[:, p * part:(p + 1) * part]
            return carry

        lax.fori_loop(0, relations, one, 0)

    for copy in w_copies:
        copy.wait()
    ag[0].wait_recv()
    transform(me_pair, 0, parts)
    forwards = []
    for j in range(1, n_pair):
        ag[j].wait_recv()
        peer = row_peers[j]
        copy = pltpu.make_async_remote_copy(
            src_ref=span(peer), dst_ref=span(peer), send_sem=fw_send.at[j], recv_sem=fw_recv.at[j],
            device_id={"row": sibling}, device_id_type=MESH,
        )
        copy.start()
        forwards.append(copy)

    sw_copy.wait()
    self_sum[...] = (
        jnp.dot(feat[...], swbuf[...], preferred_element_type=jnp.float32)
        + bias[...].reshape(1, width)
    )
    b_copy.wait()
    idx_copy.wait()
    merged[relations * slots] = jnp.zeros((block, block), merged.dtype)

    def merge_relation(r, carry):
        for s in range(slots):
            total = bbuf[r * slots + s].astype(jnp.float32)
            for t in range(s):
                same = jnp.where(pairs[r, s] == pairs[r, t], 1.0, 0.0).astype(jnp.float32)
                total = total + same * bbuf[r * slots + t].astype(jnp.float32)
            merged[r * slots + s] = total.astype(merged.dtype)
        return carry

    lax.fori_loop(0, relations, merge_relation, 0)

    orders = [list(masks) for _ in range(parts)]
    orders[1][:2] = [masks[1], masks[0]]

    def pair_of_sums(p, v, buf):
        for h in range(2):
            e = sum(
                mask * lax.rem(lax.div(v - 2 * h, 2 ** stage), 2)
                for stage, mask in enumerate(orders[p])
            )
            dest = xor(e, me_col, n_col)
            for k in range(relations * n_row):
                lhs[buf, h * block:(h + 1) * block, k * block:(k + 1) * block] = merged[idx[dest, k]]
        return jnp.dot(lhs[buf], panel[p], preferred_element_type=jnp.float32)

    base = [0]
    for _ in masks:
        base.append(base[-1] + (half >> (len(base) - 1)))

    def exchange(p, stage, slot):
        at = base[stage] + slot
        return pltpu.make_async_remote_copy(
            src_ref=sends.at[p, at], dst_ref=recvs.at[p, at],
            send_sem=rs_send.at[p, at], recv_sem=rs_recv.at[p, at],
            device_id={"col": flip(me_col, orders[p][stage])}, device_id_type=MESH,
        )

    def receive(p, stage, slot):
        exchange(p, stage, slot).wait_recv()
        return recvs[p, base[stage] + slot].astype(jnp.float32)

    def send(p, stage, slot, total):
        sends[p, base[stage] + slot] = total.astype(sends.dtype)
        exchange(p, stage, slot).start()

    for j in range(1, n_pair):
        forwards[j - 1].wait_recv()
    for p in range(parts):
        for j in range(1, n_pair):
            transform(lax.div(row_peers[j], 2), p, 1)

        def far(i, carry):
            sums = pair_of_sums(p, n_col - 1 - 4 * i, 0)
            for h in range(2):
                send(p, 0, 2 * i + h, sums[h * block:(h + 1) * block])
            return carry

        lax.fori_loop(0, half // 2, far, 0)

    def near(p, i):
        sums = pair_of_sums(p, n_col - 2 - 4 * i, (p + i) % 2)
        send(p, 1, i, sums[:block] + receive(p, 0, 2 * i))
        own[p, i] = sums[block:] + receive(p, 0, 2 * i + 1)

    def deeper(p, i):
        total = own[p, i] + receive(p, 1, i)
        stage, slot = 2, i
        while stage < len(masks) and slot % 2 == 1:
            slot = slot // 2
            total = total + receive(p, stage, slot)
            stage += 1
        if stage < len(masks):
            send(p, stage, slot // 2, total)
        else:
            at = slice(p * part, (p + 1) * part)
            out[:, at] = jnp.maximum(self_sum[:, at] + total, 0.0).astype(out.dtype)

    for i in range(half // 2):
        near(0, i)
        near(1, i)
    for p in range(2, parts):
        for i in range(half // 2):
            near(p, i)
            if p == 2 and i == 0:
                deeper(0, 0)
    for i in range(half // 2):
        for p in range(parts):
            if (p, i) != (0, 0):
                deeper(p, i)

    for copy in ag + forwards:
        copy.wait_send()
    for p in range(parts):
        for stage in range(len(masks)):
            for slot in range(half >> stage):
                exchange(p, stage, slot).wait_send()


def per_device(
    n_row, n_col,
    features, self_weight, rel_weight, bias, blocks, block_rows, block_cols, block_counts,
):
    block, width = features.shape
    relations = rel_weight.shape[1]
    slots = blocks.shape[3]
    size = blocks.shape[-1]
    bf16, f32, i32 = jnp.bfloat16, jnp.float32, jnp.int32
    vmem = pl.BlockSpec(memory_space=pltpu.VMEM)
    smem = pl.BlockSpec(memory_space=pltpu.SMEM)
    hbm = pl.BlockSpec(memory_space=pl.ANY)
    dma = pltpu.SemaphoreType.DMA
    n_src = n_row * block
    n_pair = n_row // 2
    part = 256
    lanes = pl.cdiv(relations * n_row, 128) * 128
    parts = width // part
    flops = 2 * width * (n_src * relations * width + block * width)
    flops += 2 * n_col * block * relations * n_src * width
    return pl.pallas_call(
        functools.partial(layer_kernel, n_row, n_col),
        out_shape=jax.ShapeDtypeStruct((block, width), bf16),
        in_specs=[vmem, smem, smem, smem, vmem, hbm, hbm, hbm],
        out_specs=vmem,
        scratch_shapes=[
            pltpu.VMEM((n_src, width), bf16),
            pltpu.VMEM((relations, width, width), bf16),
            pltpu.VMEM((width, width), bf16),
            pltpu.VMEM((relations * slots, size, size), bf16),
            pltpu.VMEM((relations * slots + 1, size, size), bf16),
            pltpu.VMEM((parts, relations * n_src, part), bf16),
            pltpu.VMEM((2, 2 * block, relations * n_src), bf16),
            pltpu.VMEM((n_col, lanes), i32),
            pltpu.SMEM((n_col, lanes), i32),
            pltpu.SMEM((relations, slots), i32),
            pltpu.VMEM((parts, n_col // 4, block, part), f32),
            pltpu.VMEM((block, width), f32),
            pltpu.VMEM((parts, n_col - 1, block, part), bf16),
            pltpu.VMEM((parts, n_col - 1, block, part), bf16),
            dma((relations,)), dma, dma, dma,
            dma((n_pair,)), dma((n_pair,)), dma((n_pair,)), dma((n_pair,)),
            dma((parts, n_col - 1)), dma((parts, n_col - 1)),
        ],
        compiler_params=pltpu.CompilerParams(
            collective_id=0, has_side_effects=True, vmem_limit_bytes=56 * 2 ** 20
        ),
        cost_estimate=pl.CostEstimate(flops=flops, bytes_accessed=9 * 2 ** 20, transcendentals=0),
        name="relational_layer",
    )(
        features, block_rows.reshape(relations, 1, slots), block_cols.reshape(relations, 1, slots),
        block_counts.reshape(1, relations), bias,
        jnp.transpose(rel_weight, (1, 0, 2)), self_weight,
        blocks.reshape(relations * slots, size, size),
    )


def solution(mesh):
    return jax.shard_map(
        functools.partial(per_device, mesh.shape["row"], mesh.shape["col"]),
        mesh=mesh,
        in_specs=(
            P(("row", "col"), None),
            P(),
            P(),
            P(),
            P("row", "col", None, None, None, None),
            P("row", "col", None, None),
            P("row", "col", None, None),
            P("row", "col", None),
        ),
        out_specs=P(("row", "col"), None),
        check_vma=False,
    )
```

```python
import functools

import jax
import jax.numpy as jnp
from jax import lax
from jax.experimental import pallas as pl
from jax.experimental.pallas import tpu as pltpu
from jax.sharding import PartitionSpec as P

MESH = pl.DeviceIdType.MESH


def flip(index, mask):
    out = index
    bit = 1
    while bit <= mask:
        if mask & bit:
            out = out + bit - 2 * bit * lax.rem(lax.div(index, bit), 2)
        bit *= 2
    return out


def xor(left, right, size):
    out = 0
    bit = 1
    while bit < size:
        out = out + bit * lax.rem(lax.div(left, bit) + lax.div(right, bit), 2)
        bit *= 2
    return out


def layer_kernel(
    n_row, n_col,
    feat, rows, cols, counts, bias, rel_hbm, self_hbm, blocks_hbm,
    out,
    xbuf, wbuf, swbuf, bbuf, merged, panel, lhs, table, idx, pairs, own, self_sum, sends, recvs,
    w_sem, sw_sem, b_sem, idx_sem, ag_send, ag_recv, fw_send, fw_recv, rs_send, rs_recv,
):
    block, width = feat.shape
    relations = rel_hbm.shape[0]
    slots = blocks_hbm.shape[0] // relations
    n_pair = n_row // 2
    half = n_col // 2
    n_src = n_row * block
    parts, _, part = panel.shape
    me_row = lax.axis_index("row")
    me_col = lax.axis_index("col")
    sibling = flip(me_row, 1)
    me_pair = lax.div(me_row, 2)

    barrier = pltpu.get_barrier_semaphore()
    row_peers = [sibling] + [flip(me_row, 2 * j) for j in range(1, n_pair)]
    masks = []
    while 2 ** len(masks) < n_col:
        masks.append(2 ** len(masks))
    for peer in row_peers:
        pl.semaphore_signal(barrier, inc=1, device_id={"row": peer}, device_id_type=MESH)
    for mask in masks:
        pl.semaphore_signal(
            barrier, inc=1, device_id={"col": flip(me_col, mask)}, device_id_type=MESH
        )
    b_copy = pltpu.make_async_copy(blocks_hbm, bbuf, b_sem)
    b_copy.start()
    w_copies = []
    for r in range(relations):
        copy = pltpu.make_async_copy(rel_hbm.at[r], wbuf.at[r], w_sem.at[r])
        copy.start()
        w_copies.append(copy)
    sw_copy = pltpu.make_async_copy(self_hbm, swbuf, sw_sem)
    sw_copy.start()

    pl.semaphore_wait(barrier, len(row_peers) + len(masks))

    part_rows = block // 2

    def span(row, h, many):
        at = pl.multiple_of(row * block + h * part_rows, part_rows)
        return xbuf.at[pl.ds(at, many * part_rows)]

    def gather(j, h, many):
        copy = pltpu.make_async_remote_copy(
            src_ref=feat.at[pl.ds(h * part_rows, many * part_rows)], dst_ref=span(me_row, h, many),
            send_sem=ag_send.at[j, h], recv_sem=ag_recv.at[j, h],
            device_id={"row": row_peers[j]}, device_id_type=MESH,
        )
        copy.start()
        return copy

    ag = [(j, h, gather(j, h, 1)) for j in range(1, n_pair) for h in range(2)]
    near_copy = gather(0, 0, 2)
    xbuf[pl.ds(pl.multiple_of(me_row * block, block), block), :] = feat[...]

    lane = lax.broadcasted_iota(jnp.int32, table.shape, 1)
    dest_row = lax.broadcasted_iota(jnp.int32, table.shape, 0)
    lane_relation = lax.div(lane, n_row)
    wanted = (lane_relation * n_col + dest_row) * n_row + lax.rem(lane, n_row)
    chosen = jnp.full(table.shape, relations * slots, jnp.int32)
    for r in range(relations):
        for s in range(slots):
            pair = (r * n_col + rows[r, 0, s]) * n_row + cols[r, 0, s]
            pair = jnp.where(s < counts[0, r], pair, -1)
            pairs[r, s] = pair
            chosen = jnp.where(wanted == pair, r * slots + s, chosen)
    table[...] = chosen
    idx_copy = pltpu.make_async_copy(table, idx, idx_sem)
    idx_copy.start()

    def transform(pair, first, many):
        at = pl.multiple_of(pair * 2 * block, 2 * block)

        def one(r, carry):
            product = jnp.dot(
                xbuf[pl.ds(at, 2 * block), :],
                wbuf[r, :, first * part:(first + many) * part],
                preferred_element_type=jnp.float32,
            ).astype(panel.dtype)
            to = pl.multiple_of(r * n_src + at, 2 * block)
            for p in range(many):
                panel[first + p, pl.ds(to, 2 * block), :] = product[:, p * part:(p + 1) * part]
            return carry

        lax.fori_loop(0, relations, one, 0)

    for copy in w_copies:
        copy.wait()
    near_copy.wait_recv()
    transform(me_pair, 0, parts)
    b_copy.wait()
    idx_copy.wait()
    merged[relations * slots] = jnp.zeros((block, block), merged.dtype)

    def merge_relation(r, carry):
        for s in range(slots):
            total = bbuf[r * slots + s].astype(jnp.float32)
            for t in range(s):
                same = jnp.where(pairs[r, s] == pairs[r, t], 1.0, 0.0).astype(jnp.float32)
                total = total + same * bbuf[r * slots + t].astype(jnp.float32)
            merged[r * slots + s] = total.astype(merged.dtype)
        return carry

    lax.fori_loop(0, relations, merge_relation, 0)

    forwards = []
    for j, h, copy in ag:
        copy.wait_recv()
        at = span(row_peers[j], h, 1)
        copy = pltpu.make_async_remote_copy(
            src_ref=at, dst_ref=at, send_sem=fw_send.at[j, h], recv_sem=fw_recv.at[j, h],
            device_id={"row": sibling}, device_id_type=MESH,
        )
        copy.start()
        forwards.append(copy)

    sw_copy.wait()
    self_sum[...] = (
        jnp.dot(feat[...], swbuf[...], preferred_element_type=jnp.float32)
        + bias[...].reshape(1, width)
    )
    orders = [list(masks) for _ in range(parts)]
    orders[1][:2] = [masks[1], masks[0]]

    def pair_of_sums(p, v, buf):
        for h in range(2):
            e = sum(
                mask * lax.rem(lax.div(v - 2 * h, 2 ** stage), 2)
                for stage, mask in enumerate(orders[p])
            )
            dest = xor(e, me_col, n_col)
            for k in range(relations * n_row):
                lhs[buf, h * block:(h + 1) * block, k * block:(k + 1) * block] = merged[idx[dest, k]]
        return jnp.dot(lhs[buf], panel[p], preferred_element_type=jnp.float32)

    base = [0]
    for _ in masks:
        base.append(base[-1] + (half >> (len(base) - 1)))

    def exchange(p, stage, slot):
        at = base[stage] + slot
        return pltpu.make_async_remote_copy(
            src_ref=sends.at[p, at], dst_ref=recvs.at[p, at],
            send_sem=rs_send.at[p, at], recv_sem=rs_recv.at[p, at],
            device_id={"col": flip(me_col, orders[p][stage])}, device_id_type=MESH,
        )

    def receive(p, stage, slot):
        exchange(p, stage, slot).wait_recv()
        return recvs[p, base[stage] + slot].astype(jnp.float32)

    def send(p, stage, slot, total):
        sends[p, base[stage] + slot] = total.astype(sends.dtype)
        exchange(p, stage, slot).start()

    for copy in forwards:
        copy.wait_recv()
    for p in range(parts):
        for j in range(1, n_pair):
            transform(lax.div(row_peers[j], 2), p, 1)

        def far(i, carry):
            sums = pair_of_sums(p, n_col - 1 - 4 * i, 0)
            for h in range(2):
                send(p, 0, 2 * i + h, sums[h * block:(h + 1) * block])
            return carry

        lax.fori_loop(0, half // 2, far, 0)

    def near(p, i):
        sums = pair_of_sums(p, n_col - 2 - 4 * i, (p + i) % 2)
        send(p, 1, i, sums[:block] + receive(p, 0, 2 * i))
        own[p, i] = sums[block:] + receive(p, 0, 2 * i + 1)

    def deeper(p, i):
        total = own[p, i] + receive(p, 1, i)
        stage, slot = 2, i
        while stage < len(masks) and slot % 2 == 1:
            slot = slot // 2
            total = total + receive(p, stage, slot)
            stage += 1
        if stage < len(masks):
            send(p, stage, slot // 2, total)
        else:
            at = slice(p * part, (p + 1) * part)
            out[:, at] = jnp.maximum(self_sum[:, at] + total, 0.0).astype(out.dtype)

    for i in range(half // 2):
        near(0, i)
        near(1, i)
    for p in range(2, parts):
        for i in range(half // 2):
            near(p, i)
            if p == 2 and i == 0:
                deeper(0, 0)
    for i in range(half // 2):
        for p in range(parts):
            if (p, i) != (0, 0):
                deeper(p, i)

    for copy in [near_copy] + [copy for _, _, copy in ag] + forwards:
        copy.wait_send()
    for p in range(parts):
        for stage in range(len(masks)):
            for slot in range(half >> stage):
                exchange(p, stage, slot).wait_send()


def per_device(
    n_row, n_col,
    features, self_weight, rel_weight, bias, blocks, block_rows, block_cols, block_counts,
):
    block, width = features.shape
    relations = rel_weight.shape[1]
    slots = blocks.shape[3]
    size = blocks.shape[-1]
    bf16, f32, i32 = jnp.bfloat16, jnp.float32, jnp.int32
    vmem = pl.BlockSpec(memory_space=pltpu.VMEM)
    smem = pl.BlockSpec(memory_space=pltpu.SMEM)
    hbm = pl.BlockSpec(memory_space=pl.ANY)
    dma = pltpu.SemaphoreType.DMA
    n_src = n_row * block
    n_pair = n_row // 2
    part = 256
    lanes = pl.cdiv(relations * n_row, 128) * 128
    parts = width // part
    flops = 2 * width * (n_src * relations * width + block * width)
    flops += 2 * n_col * block * relations * n_src * width
    return pl.pallas_call(
        functools.partial(layer_kernel, n_row, n_col),
        out_shape=jax.ShapeDtypeStruct((block, width), bf16),
        in_specs=[vmem, smem, smem, smem, vmem, hbm, hbm, hbm],
        out_specs=vmem,
        scratch_shapes=[
            pltpu.VMEM((n_src, width), bf16),
            pltpu.VMEM((relations, width, width), bf16),
            pltpu.VMEM((width, width), bf16),
            pltpu.VMEM((relations * slots, size, size), bf16),
            pltpu.VMEM((relations * slots + 1, size, size), bf16),
            pltpu.VMEM((parts, relations * n_src, part), bf16),
            pltpu.VMEM((2, 2 * block, relations * n_src), bf16),
            pltpu.VMEM((n_col, lanes), i32),
            pltpu.SMEM((n_col, lanes), i32),
            pltpu.SMEM((relations, slots), i32),
            pltpu.VMEM((parts, n_col // 4, block, part), f32),
            pltpu.VMEM((block, width), f32),
            pltpu.VMEM((parts, n_col - 1, block, part), bf16),
            pltpu.VMEM((parts, n_col - 1, block, part), bf16),
            dma((relations,)), dma, dma, dma,
            dma((n_pair, 2)), dma((n_pair, 2)), dma((n_pair, 2)), dma((n_pair, 2)),
            dma((parts, n_col - 1)), dma((parts, n_col - 1)),
        ],
        compiler_params=pltpu.CompilerParams(
            collective_id=0, has_side_effects=True, vmem_limit_bytes=56 * 2 ** 20
        ),
        cost_estimate=pl.CostEstimate(flops=flops, bytes_accessed=9 * 2 ** 20, transcendentals=0),
        name="relational_layer",
    )(
        features, block_rows.reshape(relations, 1, slots), block_cols.reshape(relations, 1, slots),
        block_counts.reshape(1, relations), bias,
        jnp.transpose(rel_weight, (1, 0, 2)), self_weight,
        blocks.reshape(relations * slots, size, size),
    )


def solution(mesh):
    return jax.shard_map(
        functools.partial(per_device, mesh.shape["row"], mesh.shape["col"]),
        mesh=mesh,
        in_specs=(
            P(("row", "col"), None),
            P(),
            P(),
            P(),
            P("row", "col", None, None, None, None),
            P("row", "col", None, None),
            P("row", "col", None, None),
            P("row", "col", None),
        ),
        out_specs=P(("row", "col"), None),
        check_vma=False,
    )
```

```python
import functools

import jax
import jax.numpy as jnp
from jax import lax
from jax.experimental import pallas as pl
from jax.experimental.pallas import tpu as pltpu
from jax.sharding import PartitionSpec as P

MESH = pl.DeviceIdType.MESH


def flip(index, mask):
    out = index
    bit = 1
    while bit <= mask:
        if mask & bit:
            out = out + bit - 2 * bit * lax.rem(lax.div(index, bit), 2)
        bit *= 2
    return out


def xor(left, right, size):
    out = 0
    bit = 1
    while bit < size:
        out = out + bit * lax.rem(lax.div(left, bit) + lax.div(right, bit), 2)
        bit *= 2
    return out


def layer_kernel(
    n_row, n_col,
    feat, rows, cols, counts, bias, rel_hbm, self_hbm, blocks_hbm,
    out,
    xbuf, wbuf, swbuf, bbuf, merged, panel, lhs, table, idx, pairs, own, self_sum, sends, recvs,
    w_sem, sw_sem, b_sem, idx_sem, ag_send, ag_recv, fw_send, fw_recv, rs_send, rs_recv,
):
    block, width = feat.shape
    relations = rel_hbm.shape[0]
    slots = blocks_hbm.shape[0] // relations
    n_pair = n_row // 2
    half = n_col // 2
    n_src = n_row * block
    parts, _, part = panel.shape
    me_row = lax.axis_index("row")
    me_col = lax.axis_index("col")
    sibling = flip(me_row, 1)
    me_pair = lax.div(me_row, 2)

    barrier = pltpu.get_barrier_semaphore()
    row_peers = [sibling] + [flip(me_row, 2 * j) for j in range(1, n_pair)]
    masks = []
    while 2 ** len(masks) < n_col:
        masks.append(2 ** len(masks))
    for peer in row_peers:
        pl.semaphore_signal(barrier, inc=1, device_id={"row": peer}, device_id_type=MESH)
    for mask in masks:
        pl.semaphore_signal(
            barrier, inc=1, device_id={"col": flip(me_col, mask)}, device_id_type=MESH
        )
    b_copy = pltpu.make_async_copy(blocks_hbm, bbuf, b_sem)
    b_copy.start()
    w_copies = []
    for r in range(relations):
        copy = pltpu.make_async_copy(rel_hbm.at[r], wbuf.at[r], w_sem.at[r])
        copy.start()
        w_copies.append(copy)
    sw_copy = pltpu.make_async_copy(self_hbm, swbuf, sw_sem)
    sw_copy.start()

    pl.semaphore_wait(barrier, len(row_peers) + len(masks))

    def span(row):
        return xbuf.at[pl.ds(pl.multiple_of(row * block, block), block)]

    ag = []
    for j in list(range(1, n_pair)) + [0]:
        copy = pltpu.make_async_remote_copy(
            src_ref=feat, dst_ref=span(me_row), send_sem=ag_send.at[j], recv_sem=ag_recv.at[j],
            device_id={"row": row_peers[j]}, device_id_type=MESH,
        )
        copy.start()
        ag.append(copy)
    ag = [ag[-1]] + ag[:-1]
    xbuf[pl.ds(pl.multiple_of(me_row * block, block), block), :] = feat[...]

    lane = lax.broadcasted_iota(jnp.int32, table.shape, 1)
    dest_row = lax.broadcasted_iota(jnp.int32, table.shape, 0)
    lane_relation = lax.div(lane, n_row)
    wanted = (lane_relation * n_col + dest_row) * n_row + lax.rem(lane, n_row)
    chosen = jnp.full(table.shape, relations * slots, jnp.int32)
    for r in range(relations):
        for s in range(slots):
            pair = (r * n_col + rows[r, 0, s]) * n_row + cols[r, 0, s]
            pair = jnp.where(s < counts[0, r], pair, -1)
            pairs[r, s] = pair
            chosen = jnp.where(wanted == pair, r * slots + s, chosen)
    table[...] = chosen
    idx_copy = pltpu.make_async_copy(table, idx, idx_sem)
    idx_copy.start()

    def transform(pair, first, many):
        at = pl.multiple_of(pair * 2 * block, 2 * block)

        def one(r, carry):
            product = jnp.dot(
                xbuf[pl.ds(at, 2 * block), :],
                wbuf[r, :, first * part:(first + many) * part],
                preferred_element_type=jnp.float32,
            ).astype(panel.dtype)
            to = pl.multiple_of(r * n_src + at, 2 * block)
            for p in range(many):
                panel[first + p, pl.ds(to, 2 * block), :] = product[:, p * part:(p + 1) * part]
            return carry

        lax.fori_loop(0, relations, one, 0)

    for copy in w_copies:
        copy.wait()
    ag[0].wait_recv()
    transform(me_pair, 0, parts)
    forwards = []
    for j in range(1, n_pair):
        ag[j].wait_recv()
        peer = row_peers[j]
        copy = pltpu.make_async_remote_copy(
            src_ref=span(peer), dst_ref=span(peer), send_sem=fw_send.at[j], recv_sem=fw_recv.at[j],
            device_id={"row": sibling}, device_id_type=MESH,
        )
        copy.start()
        forwards.append(copy)

    sw_copy.wait()
    self_sum[...] = (
        jnp.dot(feat[...], swbuf[...], preferred_element_type=jnp.float32)
        + bias[...].reshape(1, width)
    )
    b_copy.wait()
    idx_copy.wait()
    merged[relations * slots] = jnp.zeros((block, block), merged.dtype)

    def merge_relation(r, carry):
        for s in range(slots):
            total = bbuf[r * slots + s].astype(jnp.float32)
            for t in range(s):
                same = jnp.where(pairs[r, s] == pairs[r, t], 1.0, 0.0).astype(jnp.float32)
                total = total + same * bbuf[r * slots + t].astype(jnp.float32)
            merged[r * slots + s] = total.astype(merged.dtype)
        return carry

    lax.fori_loop(0, relations, merge_relation, 0)

    orders = [list(masks) for _ in range(parts)]
    orders[1][:2] = [masks[1], masks[0]]

    cached = lhs.shape[0] > 2

    def pair_of_sums(p, v, buf):
        own_rows = not cached or p < 2
        if cached and p == 1:
            buf = half + lax.rem(buf, 2)
        elif not cached:
            buf = lax.rem(buf, 2)
        for h in range(2 if own_rows else 0):
            e = sum(
                mask * lax.rem(lax.div(v - 2 * h, 2 ** stage), 2)
                for stage, mask in enumerate(orders[p])
            )
            dest = xor(e, me_col, n_col)
            for k in range(relations * n_row):
                lhs[buf, h * block:(h + 1) * block, k * block:(k + 1) * block] = merged[idx[dest, k]]
        return jnp.dot(lhs[buf], panel[p], preferred_element_type=jnp.float32)

    base = [0]
    for _ in masks:
        base.append(base[-1] + (half >> (len(base) - 1)))

    def exchange(p, stage, slot):
        at = base[stage] + slot
        return pltpu.make_async_remote_copy(
            src_ref=sends.at[p, at], dst_ref=recvs.at[p, at],
            send_sem=rs_send.at[p, at], recv_sem=rs_recv.at[p, at],
            device_id={"col": flip(me_col, orders[p][stage])}, device_id_type=MESH,
        )

    def receive(p, stage, slot):
        exchange(p, stage, slot).wait_recv()
        return recvs[p, base[stage] + slot].astype(jnp.float32)

    def send(p, stage, slot, total):
        sends[p, base[stage] + slot] = total.astype(sends.dtype)
        exchange(p, stage, slot).start()

    for j in range(1, n_pair):
        forwards[j - 1].wait_recv()
    for p in range(parts):
        for j in range(1, n_pair):
            transform(lax.div(row_peers[j], 2), p, 1)

        def far(i, carry):
            sums = pair_of_sums(p, n_col - 1 - 4 * i, i)
            for h in range(2):
                send(p, 0, 2 * i + h, sums[h * block:(h + 1) * block])
            return carry

        lax.fori_loop(0, half // 2, far, 0)

    def near(p, i):
        sums = pair_of_sums(p, n_col - 2 - 4 * i, half // 2 + i)
        send(p, 1, i, sums[:block] + receive(p, 0, 2 * i))
        own[p, i] = sums[block:] + receive(p, 0, 2 * i + 1)

    def deeper(p, i):
        total = own[p, i] + receive(p, 1, i)
        stage, slot = 2, i
        while stage < len(masks) and slot % 2 == 1:
            slot = slot // 2
            total = total + receive(p, stage, slot)
            stage += 1
        if stage < len(masks):
            send(p, stage, slot // 2, total)
        else:
            at = slice(p * part, (p + 1) * part)
            out[:, at] = jnp.maximum(self_sum[:, at] + total, 0.0).astype(out.dtype)

    for i in range(half // 2):
        near(0, i)
        near(1, i)
    for p in range(2, parts):
        for i in range(half // 2):
            near(p, i)
            if p == 2 and i == 0:
                deeper(0, 0)
    for i in range(half // 2):
        for p in range(parts):
            if (p, i) != (0, 0):
                deeper(p, i)

    for copy in ag + forwards:
        copy.wait_send()
    for p in range(parts):
        for stage in range(len(masks)):
            for slot in range(half >> stage):
                exchange(p, stage, slot).wait_send()


def per_device(
    n_row, n_col,
    features, self_weight, rel_weight, bias, blocks, block_rows, block_cols, block_counts,
):
    block, width = features.shape
    relations = rel_weight.shape[1]
    slots = blocks.shape[3]
    size = blocks.shape[-1]
    bf16, f32, i32 = jnp.bfloat16, jnp.float32, jnp.int32
    vmem = pl.BlockSpec(memory_space=pltpu.VMEM)
    smem = pl.BlockSpec(memory_space=pltpu.SMEM)
    hbm = pl.BlockSpec(memory_space=pl.ANY)
    dma = pltpu.SemaphoreType.DMA
    n_src = n_row * block
    n_pair = n_row // 2
    part = 256
    rows_bytes = 4 * block * relations * n_src
    buffers = n_col // 2 + 2 if (n_col // 2 + 2) * rows_bytes < 16 * 2 ** 20 else 2
    lanes = pl.cdiv(relations * n_row, 128) * 128
    parts = width // part
    flops = 2 * width * (n_src * relations * width + block * width)
    flops += 2 * n_col * block * relations * n_src * width
    return pl.pallas_call(
        functools.partial(layer_kernel, n_row, n_col),
        out_shape=jax.ShapeDtypeStruct((block, width), bf16),
        in_specs=[vmem, smem, smem, smem, vmem, hbm, hbm, hbm],
        out_specs=vmem,
        scratch_shapes=[
            pltpu.VMEM((n_src, width), bf16),
            pltpu.VMEM((relations, width, width), bf16),
            pltpu.VMEM((width, width), bf16),
            pltpu.VMEM((relations * slots, size, size), bf16),
            pltpu.VMEM((relations * slots + 1, size, size), bf16),
            pltpu.VMEM((parts, relations * n_src, part), bf16),
            pltpu.VMEM((buffers, 2 * block, relations * n_src), bf16),
            pltpu.VMEM((n_col, lanes), i32),
            pltpu.SMEM((n_col, lanes), i32),
            pltpu.SMEM((relations, slots), i32),
            pltpu.VMEM((parts, n_col // 4, block, part), f32),
            pltpu.VMEM((block, width), f32),
            pltpu.VMEM((parts, n_col - 1, block, part), bf16),
            pltpu.VMEM((parts, n_col - 1, block, part), bf16),
            dma((relations,)), dma, dma, dma,
            dma((n_pair,)), dma((n_pair,)), dma((n_pair,)), dma((n_pair,)),
            dma((parts, n_col - 1)), dma((parts, n_col - 1)),
        ],
        compiler_params=pltpu.CompilerParams(
            collective_id=0, has_side_effects=True, vmem_limit_bytes=56 * 2 ** 20
        ),
        cost_estimate=pl.CostEstimate(flops=flops, bytes_accessed=9 * 2 ** 20, transcendentals=0),
        name="relational_layer",
    )(
        features, block_rows.reshape(relations, 1, slots), block_cols.reshape(relations, 1, slots),
        block_counts.reshape(1, relations), bias,
        jnp.transpose(rel_weight, (1, 0, 2)), self_weight,
        blocks.reshape(relations * slots, size, size),
    )


def solution(mesh):
    return jax.shard_map(
        functools.partial(per_device, mesh.shape["row"], mesh.shape["col"]),
        mesh=mesh,
        in_specs=(
            P(("row", "col"), None),
            P(),
            P(),
            P(),
            P("row", "col", None, None, None, None),
            P("row", "col", None, None),
            P("row", "col", None, None),
            P("row", "col", None),
        ),
        out_specs=P(("row", "col"), None),
        check_vma=False,
    )
```
